256 devices in a mesh: rep: 4 (over z_lo), fsdp: 64 (over x, y, z_hi, core).
Axes of the slice: x: 4, y: 4, z: 8 (z_hi: 2, z_lo: 4; z = z_hi * 4 + z_lo), core: 2. Of those that a mesh axis runs over, the one named last changes fastest.
Arguments:
- hidden: bfloat16 [4, 2048, 14336], P('rep', None, 'fsdp'), may hold values from -6 to 6
- out_grad: bfloat16 [4, 2048, 4096], P('rep', None, 'fsdp'), may hold values from -0.52734375 to 0.52734375
- inner_weight: bfloat16 [4, 14336, 4096], P('rep', 'fsdp'), may hold values from -0.59765625 to 0.59765625
- adam_first: bfloat16 [4, 14336, 4096], P('rep', 'fsdp'), may hold values from -6 to 6
- adam_second: bfloat16 [4, 14336, 4096], P('rep', 'fsdp'), may hold values from 0.099609375 to 2
- anchor: float32 [14336, 4096], P('fsdp', 'rep'), may hold values from -0.6 to 0.6
- outer_momentum: float32 [14336, 4096], P('fsdp', 'rep'), may hold values from -0.3 to 0.3
Outputs:
- new_inner: bfloat16 [14336, 4096], P('fsdp')
- new_anchor: float32 [14336, 4096], P('fsdp', 'rep')
- new_momentum: float32 [14336, 4096], P('fsdp', 'rep')
- input_grad: bfloat16 [4, 2048, 14336], P('rep', None, 'fsdp')
The draws below stay inside these ranges and needn't reach their ends.
All inputs are finite; a program needn't handle non-finite values.
Results may differ from the reference program's by a relative error of at most 0.01.
Values may be sent and summed in bfloat16 or wider, within the bound.
A program may use at most 128 MiB of HBM per device.

```python
import math
import jax
import jax.numpy as jnp
from jax import lax

D = 4096
FF = 14336
TOK = 2048
REPLICAS = 4
N_REP = 4


def levels(rng, dims, cuts, least, largest):
    def one(dim, blocks):
        heights = jax.random.uniform(jax.random.fold_in(jax.random.fold_in(rng, 6), dim), (blocks,), jnp.float32, least / len(cuts), largest / len(cuts))
        return jnp.repeat(jnp.exp(heights), dims[dim] // blocks).reshape((-1,) + (1,) * (len(dims) - dim - 1))

    loudness = one(*cuts[0])
    for cut in cuts[1:]:
        loudness = loudness * one(*cut)
    return loudness


def centred(own_key, shape, width, bound, cuts=(), held_as=jnp.bfloat16):
    level = levels(own_key, shape, cuts, -0.22, 0.18) if cuts else 1.0
    result = jax.random.normal(own_key, shape, jnp.float32) * width * level
    return jnp.minimum(jnp.maximum(result, -bound), bound).astype(held_as)


def setup_inputs(seed: int = 0) -> dict:
    arg_keys = jax.random.split(jax.random.key(seed), 8)
    return {
        "hidden": centred(arg_keys[0], (REPLICAS, TOK, FF), 1.0, 6.0, ((0, 4), (2, 64))),
        "out_grad": centred(arg_keys[1], (REPLICAS, TOK, D), (4 * TOK ** -0.5), 0.52734375, ((0, 4), (2, 64))),
        "inner_weight": centred(arg_keys[2], (REPLICAS, FF, D), 0.1, 0.59765625, ((0, 4), (1, 64))),
        "adam_first": centred(arg_keys[3], (REPLICAS, FF, D), 1.0, 6.0, ((0, 4), (1, 64))),
        "adam_second": jnp.clip(jnp.exp(math.log(2.0) - 2.9996462 * jax.random.uniform(arg_keys[4], (REPLICAS, FF, D), jnp.float32) ** levels(arg_keys[4], (REPLICAS, FF, D), ((0, 4), (1, 64)), -0.2, 0.2)), 0.099609375, 2.0).astype(jnp.bfloat16),
        "anchor": centred(arg_keys[5], (FF, D), 0.1, 0.6, ((0, 64), (1, 4)), jnp.float32),
        "outer_momentum": centred(arg_keys[6], (FF, D), 0.05, 0.3, ((0, 64), (1, 4)), jnp.float32),
    }


BETA_ONE = 0.9
BETA_TWO = 0.95
INNER_RATE = 0.1
DECAY = 0.1
EPSILON = 1e-08
OUTER_RATE = 0.7
OUTER_MU = 0.9

def replica_update(activations, grads_out, weight, moment_one, moment_two):
    weight_grad = lax.dot_general(activations, grads_out, (((0,), (0,)), ((), ())), preferred_element_type=jnp.float32)
    input_back = lax.dot_general(grads_out, weight, (((1,), (1,)), ((), ())), preferred_element_type=jnp.float32)
    first = BETA_ONE * moment_one.astype(jnp.float32) + (1.0 - BETA_ONE) * weight_grad
    second = BETA_TWO * moment_two.astype(jnp.float32) + (1.0 - BETA_TWO) * weight_grad * weight_grad
    bias_one = 1.0 - BETA_ONE ** 10
    bias_two = 1.0 - BETA_TWO ** 10
    weight_full = weight.astype(jnp.float32)
    update = first / bias_one / (jnp.sqrt(second / bias_two) + EPSILON)
    stepped = weight_full - INNER_RATE * (update + DECAY * weight_full)
    return (stepped.astype(jnp.bfloat16), input_back.astype(jnp.bfloat16))

def reference(hidden, out_grad, inner_weight, adam_first, adam_second, anchor, outer_momentum):
    summed = jnp.zeros(anchor.shape, jnp.float32)
    backs = []
    for replica in range(N_REP):
        stepped, input_back = replica_update(hidden[replica], out_grad[replica], inner_weight[replica], adam_first[replica], adam_second[replica])
        summed = summed + stepped.astype(jnp.float32)
        backs.append(input_back)
    delta = anchor - summed / N_REP
    new_momentum = OUTER_MU * outer_momentum + delta
    new_anchor = anchor - OUTER_RATE * (delta + OUTER_MU * new_momentum)
    new_inner = new_anchor.astype(jnp.bfloat16)
    return (new_inner, new_anchor, new_momentum, jnp.stack(backs))
```

```python
import functools
import jax
import jax.numpy as jnp
from jax import lax
from jax.experimental import pallas as pl
from jax.experimental.pallas import tpu as pltpu
from jax.sharding import PartitionSpec as P

BETA_ONE = 0.9
BETA_TWO = 0.95
INNER_RATE = 0.1
DECAY = 0.1
EPSILON = 1e-08
OUTER_RATE = 0.7
OUTER_MU = 0.9

MESH = pl.DeviceIdType.MESH
F32 = jnp.float32
BF16 = jnp.bfloat16
UNIT = 128
LAG = 3

EVENTS = (
    (0.0, (0, 0, 0)), (4.9, (3, 0, 0)), (4.9, (1, 0, 0)), (4.9, (0, 3, 0)), (4.9, (0, 1, 0)),
    (10.6, (2, 0, 0)), (10.6, (3, 3, 0)), (10.6, (3, 1, 0)), (13.0, (0, 0, 1)), (13.5, (1, 1, 0)),
    (13.6, (1, 3, 0)), (16.3, (0, 2, 0)), (16.4, (2, 1, 0)), (18.4, (1, 0, 1)), (19.2, (3, 0, 1)),
    (20.0, (0, 1, 1)), (22.0, (2, 3, 0)), (24.1, (2, 0, 1)), (24.8, (0, 3, 1)), (24.9, (3, 2, 0)),
    (24.9, (1, 1, 1)), (27.7, (0, 2, 1)), (30.6, (3, 1, 1)), (33.4, (1, 2, 0)), (36.3, (1, 3, 1)),
    (36.3, (2, 1, 1)), (39.1, (3, 3, 1)), (39.1, (1, 2, 1)), (42.0, (3, 2, 1)), (42.0, (2, 2, 0)),
    (44.8, (2, 3, 1)), (44.8, (2, 2, 1)),
)


def plan():
    when = {key: at for at, key in EVENTS}
    ready = sorted(
        (max(when[a, b, h], when[b, a, h]), h, i) for i, (_, (a, b, h)) in enumerate(EVENTS)
    )
    units, steps, seen = [], [], 0
    for at, _, i in ready:
        units.append(EVENTS[i][1])
        now = []
        while seen < len(EVENTS) and EVENTS[seen][0] <= at:
            now.append(EVENTS[seen][1])
            seen += 1
        steps.append(now)
    return units, steps


UNITS, STEPS = plan()
N_UNITS = len(UNITS)


def packed(values, j):
    words = []
    for first in (0, 16):
        word = 0
        for i, v in enumerate(values[first : first + 16]):
            word |= v << (2 * i)
        words.append(word - (1 << 32) if word >= 1 << 31 else word)
    word = jnp.where(j < 16, jnp.int32(words[0]), jnp.int32(words[1]))
    return lax.shift_right_logical(word, 2 * lax.rem(j, 16)) & 3


def forwards(key):
    a, b, h = key
    out = []
    if key == (0, 0, 0):
        out.append("z")
    if b == 0:
        if a == 0:
            out += ["f+", "f-"]
        elif (a, h) == (3, 0):
            out.append("f+")
        elif (a, h) == (1, 1):
            out.append("f-")
        out += ["s+", "s-"]
    elif (b, h) == (3, 0):
        out.append("s+")
    elif (b, h) == (1, 1):
        out.append("s-")
    return out + ["sib"]


SENDS = {}
for _, _key in EVENTS:
    for _way in forwards(_key):
        SENDS[_key, _way] = len(SENDS)
N_SENDS = len(SENDS)


def kernel(
    h_hbm, g_hbm, w_hbm, m_hbm, v_hbm, anchor_hbm, moment_hbm,
    inner_out, anchor_out, moment_out, back_out,
    grads, acts, weight, first_m, second_m, anchor, moment,
    stepped, from_left, from_right, inner, total, back,
    load_sem, block_recv, sib_recv, block_send,
    sum_send, left_recv, right_recv, part_recv, part_left, part_right, out_sem, last_sem,
):
    rep = lax.axis_index("rep")
    place = lax.axis_index("fsdp")
    core = lax.rem(place, 2)
    zh = lax.rem(lax.div(place, 2), 2)
    y = lax.rem(lax.div(place, 4), 4)
    x = lax.div(place, 16)

    def at(px, py, ph, pc):
        return ((px * 4 + py) * 2 + ph) * 2 + pc

    def moved(a, b):
        dx = a + core * (b - a)
        dy = b + core * (a - b)
        return lax.rem(x + dx, 4), lax.rem(y + dy, 4)

    def chip(a, b):
        return at(*moved(a, b), zh, core)

    ways = {
        "f+": (rep, chip(1, 0)),
        "f-": (rep, chip(3, 0)),
        "s+": (rep, chip(0, 1)),
        "s-": (rep, chip(0, 3)),
        "z": (rep, at(x, y, 1 - zh, core)),
        "sib": (rep, at(x, y, zh, 1 - core)),
    }
    left, right = (rep - 1, place), (rep + 1, place)

    loads = [
        pltpu.make_async_copy(src, dst, load_sem.at[i])
        for i, (src, dst) in enumerate(
            (
                (g_hbm, grads.at[pl.ds(pl.multiple_of(place * 64, 64), 64)]),
                (h_hbm, acts),
                (w_hbm, weight),
                (m_hbm, first_m),
                (v_hbm, second_m),
                (anchor_hbm, anchor),
                (moment_hbm, moment),
            )
        )
    ]
    for load in loads:
        load.start()

    barrier = pltpu.get_barrier_semaphore()
    for way in ways.values():
        pl.semaphore_signal(barrier, inc=1, device_id=way, device_id_type=MESH)

    @pl.when(rep > 0)
    def _():
        pl.semaphore_signal(barrier, inc=1, device_id=left, device_id_type=MESH)

    @pl.when(rep < 3)
    def _():
        pl.semaphore_signal(barrier, inc=1, device_id=right, device_id_type=MESH)

    pl.semaphore_wait(barrier, 6 + (rep > 0).astype(jnp.int32) + (rep < 3).astype(jnp.int32))

    def unit_at(a, b, h):
        px, py = moved(a, b)
        ph = zh + h - 2 * zh * h
        return (px * 4 + py) * 2 + ph

    def block(unit, c):
        return grads.at[pl.ds(pl.multiple_of((unit * 2 + c) * 64, 64), 64)]

    def block_copy(key, way):
        unit = unit_at(*key)
        held = block(unit, core)
        recv = sib_recv if way == "sib" else block_recv
        return pltpu.make_async_remote_copy(
            src_ref=held,
            dst_ref=held,
            send_sem=block_send.at[SENDS[key, way]],
            recv_sem=recv.at[unit],
            device_id=ways[way],
            device_id_type=MESH,
        )

    def arrived(unit, c, sem):
        held = block(unit, c)
        pltpu.make_async_copy(held, held, sem.at[unit]).wait()

    def see_to(key):
        if key == (0, 0, 0):
            loads[0].wait()
        else:
            arrived(unit_at(*key), core, block_recv)
        for way in forwards(key):
            block_copy(key, way).start()

    def sum_copy(j, going_right):
        kept = from_left if going_right else from_right
        recv = left_recv if going_right else right_recv
        return pltpu.make_async_remote_copy(
            src_ref=stepped.at[j],
            dst_ref=kept.at[j],
            send_sem=sum_send.at[j],
            recv_sem=recv.at[j],
            device_id=right if going_right else left,
            device_id_type=MESH,
        )

    def part_copy(j, going_right):
        return pltpu.make_async_remote_copy(
            src_ref=inner.at[j],
            dst_ref=inner.at[j],
            send_sem=(part_right if going_right else part_left).at[j],
            recv_sem=part_recv.at[j],
            device_id=right if going_right else left,
            device_id_type=MESH,
        )

    def wait_on(ref, sem):
        pltpu.make_async_copy(ref, ref, sem).wait()

    def unit_of(j):
        a = packed([u[0] for u in UNITS], j)
        b = packed([u[1] for u in UNITS], j)
        h = packed([u[2] for u in UNITS], j)
        return unit_at(a, b, h), h

    def columns(unit):
        return pl.ds(pl.multiple_of(unit * UNIT, UNIT), UNIT)

    def out_copy(j, unit):
        return pltpu.make_async_copy(inner.at[j], inner_out.at[:, columns(unit)], out_sem.at[j])

    def adamw(j, unit):
        weight_grad = lax.dot_general(
            acts[...],
            grads[columns(unit), :],
            (((1,), (1,)), ((), ())),
            preferred_element_type=F32,
        )
        cols = columns(unit)
        weight_full = weight[:, cols].astype(F32)
        first = BETA_ONE * first_m[:, cols].astype(F32) + (1.0 - BETA_ONE) * weight_grad
        second = (
            BETA_TWO * second_m[:, cols].astype(F32)
            + (1.0 - BETA_TWO) * weight_grad * weight_grad
        )
        bias_one = 1.0 - BETA_ONE**10
        bias_two = 1.0 - BETA_TWO**10
        update = (first * (1.0 / bias_one)) / (jnp.sqrt(second * (1.0 / bias_two)) + EPSILON)
        stepped[j] = (weight_full - INNER_RATE * (update + DECAY * weight_full)).astype(BF16)

    def input_grad(unit):
        rows = pl.ds(pl.multiple_of((unit // 2) * 256, 256), 256)
        for tile in range(4):
            cols = pl.ds(tile * 512, 512)
            total[:, cols] += jnp.dot(
                weight[:, rows], grads[rows, cols], preferred_element_type=F32
            )

    def outer(j, unit, owner):
        cols = pl.ds(pl.multiple_of((unit - owner * 8) * UNIT, UNIT), UNIT)

        @pl.when(owner > 0)
        def _():
            wait_on(from_left.at[j], left_recv.at[j])

        @pl.when(owner < 3)
        def _():
            wait_on(from_right.at[j], right_recv.at[j])

        summed = stepped[j].astype(F32)
        one = jnp.where(owner > 0, from_left[j].astype(F32), 0.0)
        two = jnp.where(owner < 3, from_right[j].astype(F32), 0.0)
        mean = (summed + one + two) * 0.25
        old = anchor[:, cols]
        delta = old - mean
        moment_next = OUTER_MU * moment[:, cols] + delta
        anchor_next = old - OUTER_RATE * (delta + OUTER_MU * moment_next)
        moment[:, cols] = moment_next
        anchor[:, cols] = anchor_next
        inner[j] = anchor_next.astype(BF16)

        @pl.when(owner > 0)
        def _():
            part_copy(j, False).start()

        @pl.when(owner < 3)
        def _():
            part_copy(j, True).start()

        out_copy(j, unit).start()

    def along_rep(t):
        for hop in range(6, 0, -1):
            j = t - hop * LAG

            @pl.when((j >= 0) & (j < N_UNITS))
            def _():
                unit, _h = unit_of(j)
                owner = lax.div(unit, 8)
                last = jnp.maximum(owner, 3 - owner)
                if hop <= 3:

                    @pl.when((rep < owner) & (rep == hop))
                    def _():
                        wait_on(from_left.at[j], left_recv.at[j])
                        stepped[j] = (stepped[j].astype(F32) + from_left[j].astype(F32)).astype(BF16)
                        sum_copy(j, True).start()

                    @pl.when((rep > owner) & (3 - rep == hop))
                    def _():
                        wait_on(from_right.at[j], right_recv.at[j])
                        stepped[j] = (stepped[j].astype(F32) + from_right[j].astype(F32)).astype(BF16)
                        sum_copy(j, False).start()

                if hop in (2, 3):

                    @pl.when((rep == owner) & (last == hop))
                    def _():
                        outer(j, unit, owner)

                if hop >= 3:

                    @pl.when((rep != owner) & (last + jnp.abs(rep - owner) == hop))
                    def _():
                        wait_on(inner.at[j], part_recv.at[j])

                        @pl.when((rep < owner) & (rep > 0))
                        def _():
                            part_copy(j, False).start()

                        @pl.when((rep > owner) & (rep < 3))
                        def _():
                            part_copy(j, True).start()

                        out_copy(j, unit).start()

    def step(t, carry):
        for i, keys in enumerate(STEPS):
            if keys:

                @pl.when(t == i)
                def _():
                    for key in keys:
                        see_to(key)
                    if i == 0:
                        total[...] = jnp.zeros_like(total)
                        for load in loads[1:]:
                            load.wait()

        along_rep(t)

        @pl.when(t < N_UNITS)
        def _():
            unit, h = unit_of(t)
            owner = lax.div(unit, 8)
            arrived(unit, 1 - core, sib_recv)
            adamw(t, unit)

            @pl.when((rep == 0) & (owner > 0))
            def _():
                sum_copy(t, True).start()

            @pl.when((rep == 3) & (owner < 3))
            def _():
                sum_copy(t, False).start()

            @pl.when(h == 1)
            def _():
                input_grad(unit)

            @pl.when(t == N_UNITS - 1)
            def _():
                back[...] = total[...].astype(BF16)
                pltpu.make_async_copy(back, back_out, last_sem.at[0]).start()

        return carry

    lax.fori_loop(0, N_UNITS + 6 * LAG, step, 0)

    pltpu.make_async_copy(anchor, anchor_out, last_sem.at[1]).start()
    pltpu.make_async_copy(moment, moment_out, last_sem.at[2]).start()

    for key, way in SENDS:
        block_copy(key, way).wait_send()

    def finish(j, carry):
        unit, _h = unit_of(j)
        owner = lax.div(unit, 8)

        @pl.when(rep < owner)
        def _():
            sum_copy(j, True).wait_send()

        @pl.when(rep > owner)
        def _():
            sum_copy(j, False).wait_send()

        @pl.when((rep <= owner) & (rep > 0))
        def _():
            part_copy(j, False).wait_send()

        @pl.when((rep >= owner) & (rep < 3))
        def _():
            part_copy(j, True).wait_send()

        out_copy(j, unit).wait()
        return carry

    lax.fori_loop(0, N_UNITS, finish, 0)
    pltpu.make_async_copy(back, back_out, last_sem.at[0]).wait()
    pltpu.make_async_copy(anchor, anchor_out, last_sem.at[1]).wait()
    pltpu.make_async_copy(moment, moment_out, last_sem.at[2]).wait()


def on_device(hidden, out_grad, inner_weight, adam_first, adam_second, anchor, outer_momentum):
    acts = jnp.swapaxes(hidden[0], 0, 1)
    own = jnp.swapaxes(out_grad[0], 0, 1)
    rows, tokens = acts.shape
    width = inner_weight.shape[2]
    quarter = anchor.shape[1]
    anywhere = pl.BlockSpec(memory_space=pl.ANY)
    dma = pltpu.SemaphoreType.DMA
    slots = (N_UNITS, rows, UNIT)
    new_inner, new_anchor, new_momentum, back = pl.pallas_call(
        kernel,
        out_shape=(
            jax.ShapeDtypeStruct((rows, width), BF16),
            jax.ShapeDtypeStruct((rows, quarter), F32),
            jax.ShapeDtypeStruct((rows, quarter), F32),
            jax.ShapeDtypeStruct((rows, tokens), BF16),
        ),
        in_specs=[anywhere] * 7,
        out_specs=(anywhere,) * 4,
        scratch_shapes=[
            pltpu.VMEM((width, tokens), BF16),
            pltpu.VMEM((rows, tokens), BF16),
            pltpu.VMEM((rows, width), BF16),
            pltpu.VMEM((rows, width), BF16),
            pltpu.VMEM((rows, width), BF16),
            pltpu.VMEM((rows, quarter), F32),
            pltpu.VMEM((rows, quarter), F32),
            pltpu.VMEM(slots, BF16),
            pltpu.VMEM(slots, BF16),
            pltpu.VMEM(slots, BF16),
            pltpu.VMEM(slots, BF16),
            pltpu.VMEM((rows, tokens), F32),
            pltpu.VMEM((rows, tokens), BF16),
            dma((7,)),
            dma((N_UNITS,)),
            dma((N_UNITS,)),
            dma((N_SENDS,)),
            dma((N_UNITS,)),
            dma((N_UNITS,)),
            dma((N_UNITS,)),
            dma((N_UNITS,)),
            dma((N_UNITS,)),
            dma((N_UNITS,)),
            dma((N_UNITS,)),
            dma((3,)),
        ],
        compiler_params=pltpu.CompilerParams(
            collective_id=0, has_side_effects=True, vmem_limit_bytes=48 * 2**20
        ),
        cost_estimate=pl.CostEstimate(
            flops=4 * rows * tokens * width,
            bytes_accessed=8 * rows * width + 16 * rows * quarter + 4 * rows * tokens,
            transcendentals=rows * width,
        ),
        name="window_end",
    )(acts, own, inner_weight[0], adam_first[0], adam_second[0], anchor, outer_momentum)
    return (new_inner, new_anchor, new_momentum, jnp.swapaxes(back, 0, 1)[None])


def solution(mesh):
    placed = (
        P("rep", None, "fsdp"),
        P("rep", None, "fsdp"),
        P("rep", "fsdp", None),
        P("rep", "fsdp", None),
        P("rep", "fsdp", None),
        P("fsdp", "rep"),
        P("fsdp", "rep"),
    )
    return jax.shard_map(
        on_device,
        mesh=mesh,
        in_specs=placed,
        out_specs=(P("fsdp", None), P("fsdp", "rep"), P("fsdp", "rep"), P("rep", None, "fsdp")),
        check_vma=False,
    )
```

```python
import functools
import jax
import jax.numpy as jnp
from jax import lax
from jax.experimental import pallas as pl
from jax.experimental.pallas import tpu as pltpu
from jax.sharding import PartitionSpec as P

BETA_ONE = 0.9
BETA_TWO = 0.95
INNER_RATE = 0.1
DECAY = 0.1
EPSILON = 1e-08
OUTER_RATE = 0.7
OUTER_MU = 0.9

MESH = pl.DeviceIdType.MESH
F32 = jnp.float32
BF16 = jnp.bfloat16
UNIT = 128
LAG = 3

ARRIVALS = (
    (0, 0, 0),
    (3, 0, 0),
    (1, 0, 0),
    (0, 3, 0),
    (0, 1, 0),
    (3, 1, 0),
    (0, 0, 1),
    (2, 0, 0),
    (3, 3, 0),
    (1, 1, 0),
    (3, 0, 1),
    (1, 0, 1),
    (1, 3, 0),
    (0, 1, 1),
    (0, 2, 0),
    (2, 1, 0),
    (0, 3, 1),
    (2, 0, 1),
    (2, 3, 0),
    (3, 1, 1),
    (3, 2, 0),
    (1, 1, 1),
    (3, 3, 1),
    (0, 2, 1),
    (1, 3, 1),
    (2, 1, 1),
    (1, 2, 0),
    (3, 2, 1),
    (2, 3, 1),
    (1, 2, 1),
    (2, 2, 0),
    (2, 2, 1),
)
BEHIND = 4


def plan():
    when = {key: i for i, key in enumerate(ARRIVALS)}
    ready = sorted((max(when[a, b, h], when[b, a, h]), h, when[a, b, h]) for a, b, h in ARRIVALS)
    assert all(at <= i + BEHIND for i, (at, _, _) in enumerate(ready))
    return [ARRIVALS[i] for _, _, i in ready]


UNITS = plan()
N_UNITS = len(UNITS)
REP_HOPS = 6
STEPWISE = 24


def packed(values, j):
    words = []
    for first in (0, 16):
        word = 0
        for i, v in enumerate(values[first : first + 16]):
            word |= v << (2 * i)
        words.append(word - (1 << 32) if word >= 1 << 31 else word)
    word = jnp.where(j < 16, jnp.int32(words[0]), jnp.int32(words[1]))
    return lax.shift_right_logical(word, 2 * lax.rem(j, 16)) & 3


def forwards(key):
    a, b, h = key
    out = []
    if key == (0, 0, 0):
        out.append("z")
    if b == 0:
        if a == 0:
            out += ["f+", "f-"]
        elif (a, h) == (3, 0):
            out.append("f+")
        elif (a, h) == (1, 1):
            out.append("f-")
        out += ["s+", "s-"]
    elif (b, h) == (3, 0):
        out.append("s+")
    elif (b, h) == (1, 1):
        out.append("s-")
    return out + ["sib"]


SENDS = {}
for _key in ARRIVALS:
    for _way in forwards(_key):
        SENDS[_key, _way] = len(SENDS)
N_SENDS = len(SENDS)


def kernel(
    h_hbm, g_hbm, w_hbm, m_hbm, v_hbm, anchor_hbm, moment_hbm,
    inner_out, anchor_out, moment_out, back_out,
    grads, acts, weight, first_m, second_m, anchor, moment,
    stepped, from_near, from_far, inner, total, back,
    load_sem, block_recv, sib_recv, block_send,
    sum_send, near_recv, far_recv, part_recv, part_one, part_two, out_sem, last_sem,
):
    rep = lax.axis_index("rep")
    place = lax.axis_index("fsdp")
    core = lax.rem(place, 2)
    zh = lax.rem(lax.div(place, 2), 2)
    y = lax.rem(lax.div(place, 4), 4)
    x = lax.div(place, 16)

    def at(px, py, ph, pc):
        return ((px * 4 + py) * 2 + ph) * 2 + pc

    def moved(a, b):
        dx = a + core * (b - a)
        dy = b + core * (a - b)
        return lax.rem(x + dx, 4), lax.rem(y + dy, 4)

    def chip(a, b):
        return at(*moved(a, b), zh, core)

    ways = {
        "f+": (rep, chip(1, 0)),
        "f-": (rep, chip(3, 0)),
        "s+": (rep, chip(0, 1)),
        "s-": (rep, chip(0, 3)),
        "z": (rep, at(x, y, 1 - zh, core)),
        "sib": (rep, at(x, y, zh, 1 - core)),
    }

    loads = [
        pltpu.make_async_copy(src, dst, load_sem.at[i])
        for i, (src, dst) in enumerate(
            (
                (g_hbm, grads.at[pl.ds(pl.multiple_of(place * 64, 64), 64)]),
                (h_hbm, acts),
                (w_hbm, weight),
                (m_hbm, first_m),
                (v_hbm, second_m),
                (anchor_hbm, anchor),
                (moment_hbm, moment),
            )
        )
    ]
    for load in loads:
        load.start()

    barrier = pltpu.get_barrier_semaphore()
    for way in ways.values():
        pl.semaphore_signal(barrier, inc=1, device_id=way, device_id_type=MESH)

    for other in range(1, 4):
        pl.semaphore_signal(
            barrier, inc=1, device_id=(lax.rem(rep + other, 4), place), device_id_type=MESH
        )
    pl.semaphore_wait(barrier, 9)

    def unit_at(a, b, h):
        px, py = moved(a, b)
        ph = zh + h - 2 * zh * h
        return (px * 4 + py) * 2 + ph

    def block(unit, c):
        return grads.at[pl.ds(pl.multiple_of((unit * 2 + c) * 64, 64), 64)]

    def block_copy(key, way):
        unit = unit_at(*key)
        held = block(unit, core)
        recv = sib_recv if way == "sib" else block_recv
        return pltpu.make_async_remote_copy(
            src_ref=held,
            dst_ref=held,
            send_sem=block_send.at[SENDS[key, way]],
            recv_sem=recv.at[unit],
            device_id=ways[way],
            device_id_type=MESH,
        )

    def arrived(unit, c, sem):
        held = block(unit, c)
        pltpu.make_async_copy(held, held, sem.at[unit]).wait()

    def see_to(key):
        if key == (0, 0, 0):
            loads[0].wait()
        else:
            arrived(unit_at(*key), core, block_recv)
        for way in forwards(key):
            block_copy(key, way).start()

    def sum_copy(j, target):
        return [
            pltpu.make_async_remote_copy(
                src_ref=stepped.at[j],
                dst_ref=kept.at[j],
                send_sem=sum_send.at[j],
                recv_sem=recv.at[j],
                device_id=(target, place),
                device_id_type=MESH,
            )
            for kept, recv in ((from_near, near_recv), (from_far, far_recv))
        ]

    def part_copy(j, target, sems):
        return pltpu.make_async_remote_copy(
            src_ref=inner.at[j],
            dst_ref=inner.at[j],
            send_sem=sems.at[j],
            recv_sem=part_recv.at[j],
            device_id=(target, place),
            device_id_type=MESH,
        )

    def wait_on(ref, sem):
        pltpu.make_async_copy(ref, ref, sem).wait()

    def unit_of(j):
        a = packed([u[0] for u in UNITS], j)
        b = packed([u[1] for u in UNITS], j)
        h = packed([u[2] for u in UNITS], j)
        return unit_at(a, b, h)

    def columns(unit):
        return pl.ds(pl.multiple_of(unit * UNIT, UNIT), UNIT)

    def out_copy(j, unit):
        return pltpu.make_async_copy(inner.at[j], inner_out.at[:, columns(unit)], out_sem.at[j])

    def adamw(j, unit):
        weight_grad = lax.dot_general(
            acts[...],
            grads[columns(unit), :],
            (((1,), (1,)), ((), ())),
            preferred_element_type=F32,
        )
        cols = columns(unit)
        weight_full = weight[:, cols].astype(F32)
        first = BETA_ONE * first_m[:, cols].astype(F32) + (1.0 - BETA_ONE) * weight_grad
        second = (
            BETA_TWO * second_m[:, cols].astype(F32)
            + (1.0 - BETA_TWO) * weight_grad * weight_grad
        )
        bias_one = 1.0 - BETA_ONE**10
        bias_two = 1.0 - BETA_TWO**10
        update = (first * (1.0 / bias_one)) / (jnp.sqrt(second * (1.0 / bias_two)) + EPSILON)
        stepped[j] = (weight_full - INNER_RATE * (update + DECAY * weight_full)).astype(BF16)

    def input_grad(unit):
        rows = pl.ds(pl.multiple_of((unit // 2) * 256, 256), 256)
        for tile in range(4):
            cols = pl.ds(tile * 512, 512)
            total[:, cols] += jnp.dot(
                weight[:, rows], grads[rows, cols], preferred_element_type=F32
            )

    def roles(owner):
        low = owner < 2
        near = owner + 1 - 2 * lax.rem(owner, 2)
        return near, jnp.where(low, 2, 1), jnp.where(low, 3, 0)

    def outer(j, unit, owner, near, middle, stepwise):
        cols = pl.ds(pl.multiple_of((unit - owner * 8) * UNIT, UNIT), UNIT)
        wait_on(from_near.at[j], near_recv.at[j])

        @pl.when(jnp.logical_not(stepwise))
        def _():
            wait_on(from_far.at[j], far_recv.at[j])

        beyond = jnp.where(stepwise, 0.0, from_far[j].astype(F32))
        summed = stepped[j].astype(F32) + from_near[j].astype(F32) + beyond
        old = anchor[:, cols]
        delta = old - summed * 0.25
        moment_next = OUTER_MU * moment[:, cols] + delta
        anchor_next = old - OUTER_RATE * (delta + OUTER_MU * moment_next)
        inner[j] = anchor_next.astype(BF16)
        part_copy(j, near, part_one).start()

        @pl.when(jnp.logical_not(stepwise))
        def _():
            part_copy(j, middle, part_two).start()

        moment[:, cols] = moment_next
        anchor[:, cols] = anchor_next
        out_copy(j, unit).start()

    def line(j):
        unit = unit_of(j)
        owner = lax.div(unit, 8)
        stepwise = (j < STEPWISE) & ((owner == 0) | (owner == 3))
        return unit, owner, *roles(owner), stepwise

    def first_hop(j):
        _, owner, near, middle, far, stepwise = line(j)

        @pl.when(rep == far)
        def _():
            sum_copy(j, middle)[0].start()

        @pl.when((rep == near) & jnp.logical_not(stepwise))
        def _():
            sum_copy(j, owner)[0].start()

    def add_to(j, kept, recv):
        wait_on(kept.at[j], recv.at[j])
        stepped[j] = (stepped[j].astype(F32) + kept[j].astype(F32)).astype(BF16)

    def take_part(j, unit):
        wait_on(inner.at[j], part_recv.at[j])
        out_copy(j, unit).start()

    def along_rep(t):
        for hop in range(REP_HOPS, 0, -1):
            j = t - hop * LAG

            @pl.when((j >= 0) & (j < (STEPWISE if hop > 4 else N_UNITS)))
            def _():
                unit, owner, near, middle, far, stepwise = line(j)
                direct = jnp.logical_not(stepwise)
                if hop == 1:

                    @pl.when(rep == middle)
                    def _():
                        add_to(j, from_near, near_recv)
                        sum_copy(j, jnp.where(stepwise, near, owner))[1].start()

                if hop == 2:

                    @pl.when((rep == near) & stepwise)
                    def _():
                        add_to(j, from_far, far_recv)
                        sum_copy(j, owner)[0].start()

                if hop in (2, 3):

                    @pl.when((rep == owner) & (stepwise if hop == 3 else direct))
                    def _():
                        outer(j, unit, owner, near, middle, stepwise)

                if hop in (3, 4):

                    @pl.when((rep == near) & (stepwise if hop == 4 else direct))
                    def _():
                        take_part(j, unit)

                        @pl.when(stepwise)
                        def _():
                            part_copy(j, middle, part_one).start()

                if hop in (3, 5):

                    @pl.when((rep == middle) & (stepwise if hop == 5 else direct))
                    def _():
                        take_part(j, unit)
                        part_copy(j, far, part_one).start()

                if hop in (4, 6):

                    @pl.when((rep == far) & (stepwise if hop == 6 else direct))
                    def _():
                        take_part(j, unit)

    def step(t, carry):
        for i, key in enumerate(ARRIVALS):

            @pl.when(t == i)
            def _():
                see_to(key)

        @pl.when(t == 0)
        def _():
            total[...] = jnp.zeros_like(total)

        @pl.when(t == BEHIND)
        def _():
            for load in loads[1:]:
                load.wait()

        j = t - BEHIND
        along_rep(j)

        @pl.when((j >= 0) & (j < N_UNITS))
        def _():
            unit = unit_of(j)
            arrived(unit, 1 - core, sib_recv)
            adamw(j, unit)
            first_hop(j)

        for half in range(2):
            position = 2 * (j - N_UNITS) + half

            @pl.when((position >= 0) & (position < 16))
            def _():
                input_grad(2 * position)

        @pl.when(j == N_UNITS + 7)
        def _():
            back[...] = total[...].astype(BF16)
            pltpu.make_async_copy(back, back_out, last_sem.at[0]).start()

        return carry

    lax.fori_loop(0, BEHIND + N_UNITS + max(4 * LAG, STEPWISE - N_UNITS + 6 * LAG, 8), step, 0)

    pltpu.make_async_copy(anchor, anchor_out, last_sem.at[1]).start()
    pltpu.make_async_copy(moment, moment_out, last_sem.at[2]).start()

    for key, way in SENDS:
        block_copy(key, way).wait_send()

    def finish(j, carry):
        unit, owner, near, middle, far, stepwise = line(j)

        @pl.when(rep != owner)
        def _():
            sum_copy(j, owner)[0].wait_send()

        @pl.when((rep == owner) | (rep == middle) | ((rep == near) & stepwise))
        def _():
            part_copy(j, near, part_one).wait_send()

        @pl.when((rep == owner) & jnp.logical_not(stepwise))
        def _():
            part_copy(j, near, part_two).wait_send()

        out_copy(j, unit).wait()
        return carry

    lax.fori_loop(0, N_UNITS, finish, 0)
    pltpu.make_async_copy(back, back_out, last_sem.at[0]).wait()
    pltpu.make_async_copy(anchor, anchor_out, last_sem.at[1]).wait()
    pltpu.make_async_copy(moment, moment_out, last_sem.at[2]).wait()


def write_out(*refs):
    sems = refs[8]
    copies = [pltpu.make_async_copy(refs[i], refs[4 + i], sems.at[i]) for i in range(4)]
    for copy in copies:
        copy.start()
    for copy in copies:
        copy.wait()


def on_device(hidden, out_grad, inner_weight, adam_first, adam_second, anchor, outer_momentum):
    acts = jnp.swapaxes(hidden[0], 0, 1)
    own = jnp.swapaxes(out_grad[0], 0, 1)
    rows, tokens = acts.shape
    width = inner_weight.shape[2]
    quarter = anchor.shape[1]
    anywhere = pl.BlockSpec(memory_space=pl.ANY)
    dma = pltpu.SemaphoreType.DMA
    slots = (N_UNITS, rows, UNIT)
    results = pl.pallas_call(
        kernel,
        out_shape=(
            jax.ShapeDtypeStruct((rows, width), BF16),
            jax.ShapeDtypeStruct((rows, quarter), F32),
            jax.ShapeDtypeStruct((rows, quarter), F32),
            jax.ShapeDtypeStruct((rows, tokens), BF16),
        ),
        in_specs=[anywhere] * 7,
        out_specs=(anywhere,) * 4,
        scratch_shapes=[
            pltpu.VMEM((width, tokens), BF16),
            pltpu.VMEM((rows, tokens), BF16),
            pltpu.VMEM((rows, width), BF16),
            pltpu.VMEM((rows, width), BF16),
            pltpu.VMEM((rows, width), BF16),
            pltpu.VMEM((rows, quarter), F32),
            pltpu.VMEM((rows, quarter), F32),
            pltpu.VMEM(slots, BF16),
            pltpu.VMEM(slots, BF16),
            pltpu.VMEM(slots, BF16),
            pltpu.VMEM(slots, BF16),
            pltpu.VMEM((rows, tokens), F32),
            pltpu.VMEM((rows, tokens), BF16),
            dma((7,)),
            dma((N_UNITS,)),
            dma((N_UNITS,)),
            dma((N_SENDS,)),
            dma((N_UNITS,)),
            dma((N_UNITS,)),
            dma((N_UNITS,)),
            dma((N_UNITS,)),
            dma((N_UNITS,)),
            dma((N_UNITS,)),
            dma((N_UNITS,)),
            dma((3,)),
        ],
        compiler_params=pltpu.CompilerParams(
            collective_id=0, has_side_effects=True, vmem_limit_bytes=48 * 2**20
        ),
        cost_estimate=pl.CostEstimate(
            flops=4 * rows * tokens * width,
            bytes_accessed=8 * rows * width + 16 * rows * quarter + 4 * rows * tokens,
            transcendentals=rows * width,
        ),
        name="window_end",
    )(
        *(
            pltpu.with_memory_space_constraint(a, pltpu.HBM)
            for a in (acts, own, inner_weight[0], adam_first[0], adam_second[0], anchor, outer_momentum)
        )
    )
    new_inner, new_anchor, new_momentum, back = pl.pallas_call(
        write_out,
        out_shape=tuple(jax.ShapeDtypeStruct(r.shape, r.dtype) for r in results),
        in_specs=[anywhere] * 4,
        out_specs=(anywhere,) * 4,
        scratch_shapes=[dma((4,))],
        compiler_params=pltpu.CompilerParams(vmem_limit_bytes=2**20),
        name="write_out",
    )(*results)
    return (new_inner, new_anchor, new_momentum, jnp.swapaxes(back, 0, 1)[None])


def solution(mesh):
    placed = (
        P("rep", None, "fsdp"),
        P("rep", None, "fsdp"),
        P("rep", "fsdp", None),
        P("rep", "fsdp", None),
        P("rep", "fsdp", None),
        P("fsdp", "rep"),
        P("fsdp", "rep"),
    )
    return jax.shard_map(
        on_device,
        mesh=mesh,
        in_specs=placed,
        out_specs=(P("fsdp", None), P("fsdp", "rep"), P("fsdp", "rep"), P("rep", None, "fsdp")),
        check_vma=False,
    )
```

```python
import functools
import jax
import jax.numpy as jnp
from jax import lax
from jax.experimental import pallas as pl
from jax.experimental.pallas import tpu as pltpu
from jax.sharding import PartitionSpec as P

BETA_ONE = 0.9
BETA_TWO = 0.95
INNER_RATE = 0.1
DECAY = 0.1
EPSILON = 1e-08
OUTER_RATE = 0.7
OUTER_MU = 0.9

MESH = pl.DeviceIdType.MESH
F32 = jnp.float32
BF16 = jnp.bfloat16
UNIT = 128
LAG = 3

ARRIVALS = (
    (0, 0, 0),
    (3, 0, 0),
    (1, 0, 0),
    (0, 3, 0),
    (0, 1, 0),
    (3, 1, 0),
    (0, 0, 1),
    (2, 0, 0),
    (3, 3, 0),
    (1, 1, 0),
    (1, 3, 0),
    (0, 1, 1),
    (1, 0, 1),
    (0, 2, 0),
    (2, 1, 0),
    (3, 0, 1),
    (0, 3, 1),
    (2, 3, 0),
    (2, 0, 1),
    (0, 2, 1),
    (3, 2, 0),
    (3, 1, 1),
    (1, 2, 0),
    (1, 1, 1),
    (1, 3, 1),
    (3, 3, 1),
    (3, 2, 1),
    (2, 2, 0),
    (2, 3, 1),
    (2, 1, 1),
    (1, 2, 1),
    (2, 2, 1),
)
BEHIND = 3


def plan():
    when = {key: i for i, key in enumerate(ARRIVALS)}
    ready = sorted((max(when[a, b, h], when[b, a, h]), h, when[a, b, h]) for a, b, h in ARRIVALS)
    assert all(at <= i + BEHIND for i, (at, _, _) in enumerate(ready))
    return [ARRIVALS[i] for _, _, i in ready]


UNITS = plan()
N_UNITS = len(UNITS)
REP_HOPS = 6
STEPWISE = 26

TAIL = max(4 * LAG, STEPWISE - N_UNITS + 6 * LAG, 8)
EARLY = min(2 * TAIL, 2 * (N_UNITS - 6 * LAG) - 2)


def packed(values, j):
    words = []
    for first in (0, 16):
        word = 0
        for i, v in enumerate(values[first : first + 16]):
            word |= v << (2 * i)
        words.append(word - (1 << 32) if word >= 1 << 31 else word)
    word = jnp.where(j < 16, jnp.int32(words[0]), jnp.int32(words[1]))
    return lax.shift_right_logical(word, 2 * lax.rem(j, 16)) & 3


def forwards(key):
    a, b, h = key
    out = []
    if key == (0, 0, 0):
        out.append("z")
    if b == 0:
        if a == 0:
            out += ["f+", "f-"]
        elif (a, h) == (3, 0):
            out.append("f+")
        elif (a, h) == (1, 1):
            out.append("f-")
        out += ["s+", "s-"]
    elif (b, h) == (3, 0):
        out.append("s+")
    elif (b, h) == (1, 1):
        out.append("s-")
    return out + ["sib"]


SENDS = {}
for _key in ARRIVALS:
    for _way in forwards(_key):
        SENDS[_key, _way] = len(SENDS)
N_SENDS = len(SENDS)


def kernel(
    h_hbm, g_hbm, w_hbm, m_hbm, v_hbm, anchor_hbm, moment_hbm,
    inner_out, anchor_out, moment_out, back_out,
    grads, acts, weight, first_m, second_m, anchor, moment,
    stepped, from_near, from_far, inner, total, back,
    load_sem, block_recv, sib_recv, block_send,
    sum_send, near_recv, far_recv, part_recv, part_one, part_two, out_sem, last_sem,
):
    rep = lax.axis_index("rep")
    place = lax.axis_index("fsdp")
    core = lax.rem(place, 2)
    zh = lax.rem(lax.div(place, 2), 2)
    y = lax.rem(lax.div(place, 4), 4)
    x = lax.div(place, 16)

    def at(px, py, ph, pc):
        return ((px * 4 + py) * 2 + ph) * 2 + pc

    def moved(a, b):
        dx = a + core * (b - a)
        dy = b + core * (a - b)
        return lax.rem(x + dx, 4), lax.rem(y + dy, 4)

    def chip(a, b):
        return at(*moved(a, b), zh, core)

    ways = {
        "f+": (rep, chip(1, 0)),
        "f-": (rep, chip(3, 0)),
        "s+": (rep, chip(0, 1)),
        "s-": (rep, chip(0, 3)),
        "z": (rep, at(x, y, 1 - zh, core)),
        "sib": (rep, at(x, y, zh, 1 - core)),
    }

    loads = [
        pltpu.make_async_copy(src, dst, load_sem.at[i])
        for i, (src, dst) in enumerate(
            (
                (g_hbm, grads.at[pl.ds(pl.multiple_of(place * 64, 64), 64)]),
                (h_hbm, acts),
                (w_hbm, weight),
                (m_hbm, first_m),
                (v_hbm, second_m),
                (anchor_hbm, anchor),
                (moment_hbm, moment),
            )
        )
    ]
    for load in loads:
        load.start()

    barrier = pltpu.get_barrier_semaphore()
    for way in ways.values():
        pl.semaphore_signal(barrier, inc=1, device_id=way, device_id_type=MESH)

    for other in range(1, 4):
        pl.semaphore_signal(
            barrier, inc=1, device_id=(lax.rem(rep + other, 4), place), device_id_type=MESH
        )
    pl.semaphore_wait(barrier, 9)

    def unit_at(a, b, h):
        px, py = moved(a, b)
        ph = zh + h - 2 * zh * h
        return (px * 4 + py) * 2 + ph

    def block(unit, c):
        return grads.at[pl.ds(pl.multiple_of((unit * 2 + c) * 64, 64), 64)]

    def block_copy(key, way):
        unit = unit_at(*key)
        held = block(unit, core)
        recv = sib_recv if way == "sib" else block_recv
        return pltpu.make_async_remote_copy(
            src_ref=held,
            dst_ref=held,
            send_sem=block_send.at[SENDS[key, way]],
            recv_sem=recv.at[unit],
            device_id=ways[way],
            device_id_type=MESH,
        )

    def arrived(unit, c, sem):
        held = block(unit, c)
        pltpu.make_async_copy(held, held, sem.at[unit]).wait()

    def see_to(key):
        if key == (0, 0, 0):
            loads[0].wait()
        else:
            arrived(unit_at(*key), core, block_recv)
        for way in forwards(key):
            block_copy(key, way).start()

    def sum_copy(j, target):
        return [
            pltpu.make_async_remote_copy(
                src_ref=stepped.at[j],
                dst_ref=kept.at[j],
                send_sem=sum_send.at[j],
                recv_sem=recv.at[j],
                device_id=(target, place),
                device_id_type=MESH,
            )
            for kept, recv in ((from_near, near_recv), (from_far, far_recv))
        ]

    def part_copy(j, target, sems):
        return pltpu.make_async_remote_copy(
            src_ref=inner.at[j],
            dst_ref=inner.at[j],
            send_sem=sems.at[j],
            recv_sem=part_recv.at[j],
            device_id=(target, place),
            device_id_type=MESH,
        )

    def wait_on(ref, sem):
        pltpu.make_async_copy(ref, ref, sem).wait()

    def unit_of(j):
        a = packed([u[0] for u in UNITS], j)
        b = packed([u[1] for u in UNITS], j)
        h = packed([u[2] for u in UNITS], j)
        return unit_at(a, b, h)

    def columns(unit):
        return pl.ds(pl.multiple_of(unit * UNIT, UNIT), UNIT)

    def out_copy(j, unit):
        return pltpu.make_async_copy(inner.at[j], inner_out.at[:, columns(unit)], out_sem.at[j])

    def adamw(j, unit):
        weight_grad = lax.dot_general(
            acts[...],
            grads[columns(unit), :],
            (((1,), (1,)), ((), ())),
            preferred_element_type=F32,
        )
        cols = columns(unit)
        weight_full = weight[:, cols].astype(F32)
        first = BETA_ONE * first_m[:, cols].astype(F32) + (1.0 - BETA_ONE) * weight_grad
        second = (
            BETA_TWO * second_m[:, cols].astype(F32)
            + (1.0 - BETA_TWO) * weight_grad * weight_grad
        )
        bias_one = 1.0 - BETA_ONE**10
        bias_two = 1.0 - BETA_TWO**10
        update = (first * (1.0 / bias_one)) / (jnp.sqrt(second * (1.0 / bias_two)) + EPSILON)
        stepped[j] = (weight_full - INNER_RATE * (update + DECAY * weight_full)).astype(BF16)

    def input_grad(unit):
        rows = pl.ds(pl.multiple_of((unit // 2) * 256, 256), 256)
        for tile in range(4):
            cols = pl.ds(tile * 512, 512)
            total[:, cols] += jnp.dot(
                weight[:, rows], grads[rows, cols], preferred_element_type=F32
            )

    def roles(owner):
        low = owner < 2
        near = owner ^ 1
        return near, jnp.where(low, 2, 1), jnp.where(low, 3, 0)

    def outer(j, unit, owner, near, middle, stepwise):
        cols = pl.ds(pl.multiple_of((unit - owner * 8) * UNIT, UNIT), UNIT)
        wait_on(from_near.at[j], near_recv.at[j])

        @pl.when(jnp.logical_not(stepwise))
        def _():
            wait_on(from_far.at[j], far_recv.at[j])

        beyond = jnp.where(stepwise, 0.0, from_far[j].astype(F32))
        summed = stepped[j].astype(F32) + from_near[j].astype(F32) + beyond
        old = anchor[:, cols]
        delta = old - summed * 0.25
        moment_next = OUTER_MU * moment[:, cols] + delta
        anchor_next = old - OUTER_RATE * (delta + OUTER_MU * moment_next)
        inner[j] = anchor_next.astype(BF16)
        part_copy(j, near, part_one).start()

        @pl.when(jnp.logical_not(stepwise))
        def _():
            part_copy(j, middle, part_two).start()

        moment[:, cols] = moment_next
        anchor[:, cols] = anchor_next
        out_copy(j, unit).start()

    def line(j, unit):
        owner = unit >> 3
        stepwise = (j < STEPWISE) & ((owner == 0) | (owner == 3))
        return owner, *roles(owner), stepwise

    def first_hop(j, unit):
        owner, near, middle, far, stepwise = line(j, unit)

        @pl.when(rep == far)
        def _():
            sum_copy(j, middle)[0].start()

        @pl.when((rep == near) & jnp.logical_not(stepwise))
        def _():
            sum_copy(j, owner)[0].start()

    def add_to(j, kept, recv):
        wait_on(kept.at[j], recv.at[j])
        stepped[j] = (stepped[j].astype(F32) + kept[j].astype(F32)).astype(BF16)

    def take_part(j, unit):
        wait_on(inner.at[j], part_recv.at[j])
        out_copy(j, unit).start()

    def along_rep(t, units):
        for hop in range(REP_HOPS, 0, -1):
            j = t - hop * LAG

            @pl.when((j >= 0) & (j < (STEPWISE if hop > 4 else N_UNITS)))
            def _():
                unit = units[hop * LAG - 1]
                owner, near, middle, far, stepwise = line(j, unit)
                direct = jnp.logical_not(stepwise)
                if hop == 1:

                    @pl.when(rep == middle)
                    def _():
                        add_to(j, from_near, near_recv)
                        sum_copy(j, jnp.where(stepwise, near, owner))[1].start()

                if hop == 2:

                    @pl.when((rep == near) & stepwise)
                    def _():
                        add_to(j, from_far, far_recv)
                        sum_copy(j, owner)[0].start()

                if hop in (2, 3):

                    @pl.when((rep == owner) & (stepwise if hop == 3 else direct))
                    def _():
                        outer(j, unit, owner, near, middle, stepwise)

                if hop in (3, 4):

                    @pl.when((rep == near) & (stepwise if hop == 4 else direct))
                    def _():
                        take_part(j, unit)

                        @pl.when(stepwise)
                        def _():
                            part_copy(j, middle, part_one).start()

                if hop in (3, 5):

                    @pl.when((rep == middle) & (stepwise if hop == 5 else direct))
                    def _():
                        take_part(j, unit)
                        part_copy(j, far, part_one).start()

                if hop in (4, 6):

                    @pl.when((rep == far) & (stepwise if hop == 6 else direct))
                    def _():
                        take_part(j, unit)

    def step(t, units):
        for i, key in enumerate(ARRIVALS):

            @pl.when(t == i)
            def _():
                see_to(key)

        @pl.when(t == 0)
        def _():
            total[...] = jnp.zeros_like(total)

        @pl.when(t == BEHIND)
        def _():
            for load in loads[1:]:
                load.wait()

        j = t - BEHIND
        along_rep(j, units)
        unit = unit_of(jnp.minimum(jnp.maximum(j, 0), N_UNITS - 1))

        @pl.when((j >= 0) & (j < N_UNITS))
        def _():
            arrived(unit, 1 - core, sib_recv)
            adamw(j, unit)
            first_hop(j, unit)

        for half in range(2):
            position = 2 * (j - N_UNITS) + half

            @pl.when((position >= 0) & (position < 16))
            def _():
                input_grad(2 * position)

        @pl.when(j == N_UNITS + 7)
        def _():
            back[...] = total[...].astype(BF16)
            pltpu.make_async_copy(back, back_out, last_sem.at[0]).start()

        @pl.when(j == N_UNITS + 3 * LAG - 1)
        def _():
            pltpu.make_async_copy(anchor, anchor_out, last_sem.at[1]).start()
            pltpu.make_async_copy(moment, moment_out, last_sem.at[2]).start()

        @pl.when(j == N_UNITS + 2 * LAG)
        def _():
            for key, way in SENDS:
                block_copy(key, way).wait_send()

        for half in range(2):
            old = 2 * (j - N_UNITS) + half

            @pl.when((old >= 0) & (old < EARLY))
            def _():
                finish(old, 0)

        return (unit, *units[:-1])

    def finish(j, carry):
        unit = unit_of(j)
        owner, near, middle, far, stepwise = line(j, unit)

        @pl.when(rep != owner)
        def _():
            sum_copy(j, owner)[0].wait_send()

        @pl.when((rep == owner) | (rep == middle) | ((rep == near) & stepwise))
        def _():
            part_copy(j, near, part_one).wait_send()

        @pl.when((rep == owner) & jnp.logical_not(stepwise))
        def _():
            part_copy(j, near, part_two).wait_send()

        out_copy(j, unit).wait()
        return carry

    lax.fori_loop(0, BEHIND + N_UNITS + TAIL, step, (jnp.int32(0),) * (6 * LAG))
    lax.fori_loop(EARLY, N_UNITS, finish, 0)
    pltpu.make_async_copy(back, back_out, last_sem.at[0]).wait()
    pltpu.make_async_copy(anchor, anchor_out, last_sem.at[1]).wait()
    pltpu.make_async_copy(moment, moment_out, last_sem.at[2]).wait()


def write_out(*refs):
    sems = refs[8]
    copies = []
    for i in range(4):
        half = refs[i].shape[0] // 2
        for rows in (pl.ds(0, half), pl.ds(half, half)):
            copies.append(
                pltpu.make_async_copy(refs[i].at[rows], refs[4 + i].at[rows], sems.at[len(copies)])
            )
    for copy in copies:
        copy.start()
    for copy in copies:
        copy.wait()


def on_device(hidden, out_grad, inner_weight, adam_first, adam_second, anchor, outer_momentum):
    acts = jnp.swapaxes(hidden[0], 0, 1)
    own = jnp.swapaxes(out_grad[0], 0, 1)
    rows, tokens = acts.shape
    width = inner_weight.shape[2]
    quarter = anchor.shape[1]
    anywhere = pl.BlockSpec(memory_space=pl.ANY)
    dma = pltpu.SemaphoreType.DMA
    slots = (N_UNITS, rows, UNIT)
    results = pl.pallas_call(
        kernel,
        out_shape=(
            jax.ShapeDtypeStruct((rows, width), BF16),
            jax.ShapeDtypeStruct((rows, quarter), F32),
            jax.ShapeDtypeStruct((rows, quarter), F32),
            jax.ShapeDtypeStruct((rows, tokens), BF16),
        ),
        in_specs=[anywhere] * 7,
        out_specs=(anywhere,) * 4,
        scratch_shapes=[
            pltpu.VMEM((width, tokens), BF16),
            pltpu.VMEM((rows, tokens), BF16),
            pltpu.VMEM((rows, width), BF16),
            pltpu.VMEM((rows, width), BF16),
            pltpu.VMEM((rows, width), BF16),
            pltpu.VMEM((rows, quarter), F32),
            pltpu.VMEM((rows, quarter), F32),
            pltpu.VMEM(slots, BF16),
            pltpu.VMEM(slots, BF16),
            pltpu.VMEM(slots, BF16),
            pltpu.VMEM(slots, BF16),
            pltpu.VMEM((rows, tokens), F32),
            pltpu.VMEM((rows, tokens), BF16),
            dma((7,)),
            dma((N_UNITS,)),
            dma((N_UNITS,)),
            dma((N_SENDS,)),
            dma((N_UNITS,)),
            dma((N_UNITS,)),
            dma((N_UNITS,)),
            dma((N_UNITS,)),
            dma((N_UNITS,)),
            dma((N_UNITS,)),
            dma((N_UNITS,)),
            dma((3,)),
        ],
        compiler_params=pltpu.CompilerParams(
            collective_id=0, has_side_effects=True, vmem_limit_bytes=48 * 2**20
        ),
        cost_estimate=pl.CostEstimate(
            flops=4 * rows * tokens * width,
            bytes_accessed=8 * rows * width + 16 * rows * quarter + 4 * rows * tokens,
            transcendentals=rows * width,
        ),
        name="window_end",
    )(
        *(
            pltpu.with_memory_space_constraint(a, pltpu.HBM)
            for a in (acts, own, inner_weight[0], adam_first[0], adam_second[0], anchor, outer_momentum)
        )
    )
    new_inner, new_anchor, new_momentum, back = pl.pallas_call(
        write_out,
        out_shape=tuple(jax.ShapeDtypeStruct(r.shape, r.dtype) for r in results),
        in_specs=[anywhere] * 4,
        out_specs=(anywhere,) * 4,
        scratch_shapes=[dma((8,))],
        compiler_params=pltpu.CompilerParams(vmem_limit_bytes=2**20),
        name="write_out",
    )(*results)
    return (new_inner, new_anchor, new_momentum, jnp.swapaxes(back, 0, 1)[None])


def solution(mesh):
    placed = (
        P("rep", None, "fsdp"),
        P("rep", None, "fsdp"),
        P("rep", "fsdp", None),
        P("rep", "fsdp", None),
        P("rep", "fsdp", None),
        P("fsdp", "rep"),
        P("fsdp", "rep"),
    )
    return jax.shard_map(
        on_device,
        mesh=mesh,
        in_specs=placed,
        out_specs=(P("fsdp", None), P("fsdp", "rep"), P("fsdp", "rep"), P("rep", None, "fsdp")),
        check_vma=False,
    )
```

```python
import functools
import jax
import jax.numpy as jnp
from jax import lax
from jax.experimental import pallas as pl
from jax.experimental.pallas import tpu as pltpu
from jax.sharding import PartitionSpec as P

BETA_ONE = 0.9
BETA_TWO = 0.95
INNER_RATE = 0.1
DECAY = 0.1
EPSILON = 1e-08
OUTER_RATE = 0.7
OUTER_MU = 0.9

MESH = pl.DeviceIdType.MESH
F32 = jnp.float32
BF16 = jnp.bfloat16
UNIT = 128
HOPS = (3, 6, 9, 12, 15, 18)

ARRIVALS = (
    (0, 0, 0),
    (3, 0, 0),
    (1, 0, 0),
    (0, 3, 0),
    (0, 1, 0),
    (3, 1, 0),
    (0, 0, 1),
    (2, 0, 0),
    (3, 3, 0),
    (1, 1, 0),
    (1, 3, 0),
    (0, 1, 1),
    (1, 0, 1),
    (0, 2, 0),
    (2, 1, 0),
    (3, 0, 1),
    (0, 3, 1),
    (2, 3, 0),
    (2, 0, 1),
    (0, 2, 1),
    (3, 2, 0),
    (3, 1, 1),
    (1, 2, 0),
    (1, 1, 1),
    (1, 3, 1),
    (3, 3, 1),
    (3, 2, 1),
    (2, 2, 0),
    (2, 3, 1),
    (2, 1, 1),
    (1, 2, 1),
    (2, 2, 1),
)
BEHIND = 3


def plan():
    when = {key: i for i, key in enumerate(ARRIVALS)}
    ready = sorted((max(when[a, b, h], when[b, a, h]), h, when[a, b, h]) for a, b, h in ARRIVALS)
    assert all(at <= i + BEHIND for i, (at, _, _) in enumerate(ready))
    return [ARRIVALS[i] for _, _, i in ready]


UNITS = plan()
N_UNITS = len(UNITS)
STEPWISE = 25

TAIL = max(HOPS[3], STEPWISE - N_UNITS + HOPS[5], 8)
EARLY = min(2 * TAIL, 2 * (N_UNITS - HOPS[5]) - 2)


def packed(values, j):
    words = []
    for first in (0, 16):
        word = 0
        for i, v in enumerate(values[first : first + 16]):
            word |= v << (2 * i)
        words.append(word - (1 << 32) if word >= 1 << 31 else word)
    word = jnp.where(j < 16, jnp.int32(words[0]), jnp.int32(words[1]))
    return lax.shift_right_logical(word, 2 * lax.rem(j, 16)) & 3


def forwards(key):
    a, b, h = key
    out = []
    if key == (0, 0, 0):
        out.append("z")
    if b == 0:
        if a == 0:
            out += ["f+", "f-"]
        elif (a, h) == (3, 0):
            out.append("f+")
        elif (a, h) == (1, 1):
            out.append("f-")
        out += ["s+", "s-"]
    elif (b, h) == (3, 0):
        out.append("s+")
    elif (b, h) == (1, 1):
        out.append("s-")
    return out + ["sib"]


SENDS = {}
for _key in ARRIVALS:
    for _way in forwards(_key):
        SENDS[_key, _way] = len(SENDS)
N_SENDS = len(SENDS)


def kernel(
    h_hbm, g_hbm, w_hbm, m_hbm, v_hbm, anchor_hbm, moment_hbm,
    inner_out, anchor_out, moment_out, back_out,
    grads, acts, weight, first_m, second_m, anchor, moment,
    stepped, from_near, from_far, inner, total, back,
    load_sem, block_recv, sib_recv, block_send,
    sum_send, near_recv, far_recv, part_recv, part_one, part_two, out_sem, last_sem,
):
    rep = lax.axis_index("rep")
    place = lax.axis_index("fsdp")
    core = lax.rem(place, 2)
    zh = lax.rem(lax.div(place, 2), 2)
    y = lax.rem(lax.div(place, 4), 4)
    x = lax.div(place, 16)

    def at(px, py, ph, pc):
        return ((px * 4 + py) * 2 + ph) * 2 + pc

    def moved(a, b):
        dx = a + core * (b - a)
        dy = b + core * (a - b)
        return lax.rem(x + dx, 4), lax.rem(y + dy, 4)

    def chip(a, b):
        return at(*moved(a, b), zh, core)

    ways = {
        "f+": (rep, chip(1, 0)),
        "f-": (rep, chip(3, 0)),
        "s+": (rep, chip(0, 1)),
        "s-": (rep, chip(0, 3)),
        "z": (rep, at(x, y, 1 - zh, core)),
        "sib": (rep, at(x, y, zh, 1 - core)),
    }

    loads = [
        pltpu.make_async_copy(src, dst, load_sem.at[i])
        for i, (src, dst) in enumerate(
            (
                (g_hbm, grads.at[pl.ds(pl.multiple_of(place * 64, 64), 64)]),
                (h_hbm, acts),
                (w_hbm, weight),
                (m_hbm, first_m),
                (v_hbm, second_m),
                (anchor_hbm, anchor),
                (moment_hbm, moment),
            )
        )
    ]
    barrier = pltpu.get_barrier_semaphore()
    for way in ways.values():
        pl.semaphore_signal(barrier, inc=1, device_id=way, device_id_type=MESH)

    for other in range(1, 4):
        pl.semaphore_signal(
            barrier, inc=1, device_id=(lax.rem(rep + other, 4), place), device_id_type=MESH
        )
    for load in loads:
        load.start()

    pl.semaphore_wait(barrier, 9)

    def unit_at(a, b, h):
        px, py = moved(a, b)
        ph = zh + h - 2 * zh * h
        return (px * 4 + py) * 2 + ph

    def block(unit, c):
        return grads.at[pl.ds(pl.multiple_of((unit * 2 + c) * 64, 64), 64)]

    def block_copy(key, way):
        unit = unit_at(*key)
        held = block(unit, core)
        recv = sib_recv if way == "sib" else block_recv
        return pltpu.make_async_remote_copy(
            src_ref=held,
            dst_ref=held,
            send_sem=block_send.at[SENDS[key, way]],
            recv_sem=recv.at[unit],
            device_id=ways[way],
            device_id_type=MESH,
        )

    def arrived(unit, c, sem):
        held = block(unit, c)
        pltpu.make_async_copy(held, held, sem.at[unit]).wait()

    def see_to(key):
        if key == (0, 0, 0):
            loads[0].wait()
        else:
            arrived(unit_at(*key), core, block_recv)
        for way in forwards(key):
            block_copy(key, way).start()

    def sum_copy(j, target):
        return [
            pltpu.make_async_remote_copy(
                src_ref=stepped.at[j],
                dst_ref=kept.at[j],
                send_sem=sum_send.at[j],
                recv_sem=recv.at[j],
                device_id=(target, place),
                device_id_type=MESH,
            )
            for kept, recv in ((from_near, near_recv), (from_far, far_recv))
        ]

    def part_copy(j, target, sems):
        return pltpu.make_async_remote_copy(
            src_ref=inner.at[j],
            dst_ref=inner.at[j],
            send_sem=sems.at[j],
            recv_sem=part_recv.at[j],
            device_id=(target, place),
            device_id_type=MESH,
        )

    def wait_on(ref, sem):
        pltpu.make_async_copy(ref, ref, sem).wait()

    def unit_of(j):
        a = packed([u[0] for u in UNITS], j)
        b = packed([u[1] for u in UNITS], j)
        h = packed([u[2] for u in UNITS], j)
        return unit_at(a, b, h)

    def columns(unit):
        return pl.ds(pl.multiple_of(unit * UNIT, UNIT), UNIT)

    def out_copy(j, unit):
        return pltpu.make_async_copy(inner.at[j], inner_out.at[:, columns(unit)], out_sem.at[j])

    def adamw(j, unit):
        weight_grad = lax.dot_general(
            acts[...],
            grads[columns(unit), :],
            (((1,), (1,)), ((), ())),
            preferred_element_type=F32,
        )
        cols = columns(unit)
        weight_full = weight[:, cols].astype(F32)
        first = BETA_ONE * first_m[:, cols].astype(F32) + (1.0 - BETA_ONE) * weight_grad
        second = (
            BETA_TWO * second_m[:, cols].astype(F32)
            + (1.0 - BETA_TWO) * weight_grad * weight_grad
        )
        bias_one = 1.0 - BETA_ONE**10
        bias_two = 1.0 - BETA_TWO**10
        update = (first * (1.0 / bias_one)) / (jnp.sqrt(second * (1.0 / bias_two)) + EPSILON)
        stepped[j] = (weight_full - INNER_RATE * (update + DECAY * weight_full)).astype(BF16)

    def input_grad(unit):
        rows = pl.ds(pl.multiple_of((unit // 2) * 256, 256), 256)
        for tile in range(4):
            cols = pl.ds(tile * 512, 512)
            total[:, cols] += jnp.dot(
                weight[:, rows], grads[rows, cols], preferred_element_type=F32
            )

    def roles(owner):
        low = owner < 2
        near = owner ^ 1
        return near, jnp.where(low, 2, 1), jnp.where(low, 3, 0)

    def outer(j, unit, owner, near, middle, stepwise):
        cols = pl.ds(pl.multiple_of((unit - owner * 8) * UNIT, UNIT), UNIT)
        wait_on(from_near.at[j], near_recv.at[j])

        @pl.when(jnp.logical_not(stepwise))
        def _():
            wait_on(from_far.at[j], far_recv.at[j])

        beyond = jnp.where(stepwise, 0.0, from_far[j].astype(F32))
        summed = stepped[j].astype(F32) + from_near[j].astype(F32) + beyond
        old = anchor[:, cols]
        delta = old - summed * 0.25
        moment_next = OUTER_MU * moment[:, cols] + delta
        anchor_next = old - OUTER_RATE * (delta + OUTER_MU * moment_next)
        inner[j] = anchor_next.astype(BF16)
        part_copy(j, near, part_one).start()

        @pl.when(jnp.logical_not(stepwise))
        def _():
            part_copy(j, middle, part_two).start()

        moment[:, cols] = moment_next
        anchor[:, cols] = anchor_next
        out_copy(j, unit).start()

    def line(j, unit):
        owner = unit >> 3
        stepwise = (j < STEPWISE) & ((owner == 0) | (owner == 3))
        return owner, *roles(owner), stepwise

    def first_hop(j, unit):
        owner, near, middle, far, stepwise = line(j, unit)

        @pl.when(rep == far)
        def _():
            sum_copy(j, middle)[0].start()

        @pl.when((rep == near) & jnp.logical_not(stepwise))
        def _():
            sum_copy(j, owner)[0].start()

    def add_to(j, kept, recv):
        wait_on(kept.at[j], recv.at[j])
        stepped[j] = (stepped[j].astype(F32) + kept[j].astype(F32)).astype(BF16)

    def take_part(j, unit):
        wait_on(inner.at[j], part_recv.at[j])
        out_copy(j, unit).start()

    def along_rep(t, units):
        for hop in range(6, 0, -1):
            j = t - HOPS[hop - 1]

            @pl.when((j >= 0) & (j < (STEPWISE if hop > 4 else N_UNITS)))
            def _():
                unit = units[HOPS[hop - 1] - 1]
                owner, near, middle, far, stepwise = line(j, unit)
                direct = jnp.logical_not(stepwise)
                if hop == 1:

                    @pl.when(rep == middle)
                    def _():
                        add_to(j, from_near, near_recv)
                        sum_copy(j, jnp.where(stepwise, near, owner))[1].start()

                if hop == 2:

                    @pl.when((rep == near) & stepwise)
                    def _():
                        add_to(j, from_far, far_recv)
                        sum_copy(j, owner)[0].start()

                if hop in (2, 3):

                    @pl.when((rep == owner) & (stepwise if hop == 3 else direct))
                    def _():
                        outer(j, unit, owner, near, middle, stepwise)

                if hop in (3, 4):

                    @pl.when((rep == near) & (stepwise if hop == 4 else direct))
                    def _():
                        take_part(j, unit)

                        @pl.when(stepwise)
                        def _():
                            part_copy(j, middle, part_one).start()

                if hop in (3, 5):

                    @pl.when((rep == middle) & (stepwise if hop == 5 else direct))
                    def _():
                        take_part(j, unit)
                        part_copy(j, far, part_one).start()

                if hop in (4, 6):

                    @pl.when((rep == far) & (stepwise if hop == 6 else direct))
                    def _():
                        take_part(j, unit)

    def step(t, units):
        for i, key in enumerate(ARRIVALS):

            @pl.when(t == i)
            def _():
                see_to(key)

        @pl.when(t == 0)
        def _():
            total[...] = jnp.zeros_like(total)

        @pl.when(t == BEHIND)
        def _():
            for load in loads[1:]:
                load.wait()

        j = t - BEHIND
        along_rep(j, units)
        unit = unit_of(jnp.minimum(jnp.maximum(j, 0), N_UNITS - 1))

        @pl.when((j >= 0) & (j < N_UNITS))
        def _():
            arrived(unit, 1 - core, sib_recv)
            adamw(j, unit)
            first_hop(j, unit)

        for half in range(2):
            position = 2 * (j - N_UNITS) + half

            @pl.when((position >= 0) & (position < 16))
            def _():
                input_grad(2 * position)

        @pl.when(j == N_UNITS + 7)
        def _():
            back[...] = total[...].astype(BF16)
            pltpu.make_async_copy(back, back_out, last_sem.at[0]).start()

        @pl.when(j == N_UNITS + HOPS[2] - 1)
        def _():
            pltpu.make_async_copy(anchor, anchor_out, last_sem.at[1]).start()
            pltpu.make_async_copy(moment, moment_out, last_sem.at[2]).start()

        @pl.when(j == N_UNITS + HOPS[1])
        def _():
            for key, way in SENDS:
                block_copy(key, way).wait_send()

        for half in range(2):
            old = 2 * (j - N_UNITS) + half

            @pl.when((old >= 0) & (old < EARLY))
            def _():
                finish(old, 0)

        return (unit, *units[:-1])

    def finish(j, carry):
        unit = unit_of(j)
        owner, near, middle, far, stepwise = line(j, unit)

        @pl.when(rep != owner)
        def _():
            sum_copy(j, owner)[0].wait_send()

        @pl.when((rep == owner) | (rep == middle) | ((rep == near) & stepwise))
        def _():
            part_copy(j, near, part_one).wait_send()

        @pl.when((rep == owner) & jnp.logical_not(stepwise))
        def _():
            part_copy(j, near, part_two).wait_send()

        out_copy(j, unit).wait()
        return carry

    lax.fori_loop(0, BEHIND + N_UNITS + TAIL, step, (jnp.int32(0),) * HOPS[5])
    lax.fori_loop(EARLY, N_UNITS, finish, 0)
    pltpu.make_async_copy(back, back_out, last_sem.at[0]).wait()
    pltpu.make_async_copy(anchor, anchor_out, last_sem.at[1]).wait()
    pltpu.make_async_copy(moment, moment_out, last_sem.at[2]).wait()


def write_out(*refs):
    sems = refs[8]
    copies = []
    for i in range(4):
        half = refs[i].shape[0] // 2
        for rows in (pl.ds(0, half), pl.ds(half, half)):
            copies.append(
                pltpu.make_async_copy(refs[i].at[rows], refs[4 + i].at[rows], sems.at[len(copies)])
            )
    for copy in copies:
        copy.start()
    for copy in copies:
        copy.wait()


def on_device(hidden, out_grad, inner_weight, adam_first, adam_second, anchor, outer_momentum):
    acts = jnp.swapaxes(hidden[0], 0, 1)
    own = jnp.swapaxes(out_grad[0], 0, 1)
    rows, tokens = acts.shape
    width = inner_weight.shape[2]
    quarter = anchor.shape[1]
    anywhere = pl.BlockSpec(memory_space=pl.ANY)
    dma = pltpu.SemaphoreType.DMA
    slots = (N_UNITS, rows, UNIT)
    results = pl.pallas_call(
        kernel,
        out_shape=(
            jax.ShapeDtypeStruct((rows, width), BF16),
            jax.ShapeDtypeStruct((rows, quarter), F32),
            jax.ShapeDtypeStruct((rows, quarter), F32),
            jax.ShapeDtypeStruct((rows, tokens), BF16),
        ),
        in_specs=[anywhere] * 7,
        out_specs=(anywhere,) * 4,
        scratch_shapes=[
            pltpu.VMEM((width, tokens), BF16),
            pltpu.VMEM((rows, tokens), BF16),
            pltpu.VMEM((rows, width), BF16),
            pltpu.VMEM((rows, width), BF16),
            pltpu.VMEM((rows, width), BF16),
            pltpu.VMEM((rows, quarter), F32),
            pltpu.VMEM((rows, quarter), F32),
            pltpu.VMEM(slots, BF16),
            pltpu.VMEM(slots, BF16),
            pltpu.VMEM(slots, BF16),
            pltpu.VMEM(slots, BF16),
            pltpu.VMEM((rows, tokens), F32),
            pltpu.VMEM((rows, tokens), BF16),
            dma((7,)),
            dma((N_UNITS,)),
            dma((N_UNITS,)),
            dma((N_SENDS,)),
            dma((N_UNITS,)),
            dma((N_UNITS,)),
            dma((N_UNITS,)),
            dma((N_UNITS,)),
            dma((N_UNITS,)),
            dma((N_UNITS,)),
            dma((N_UNITS,)),
            dma((3,)),
        ],
        compiler_params=pltpu.CompilerParams(
            collective_id=0, has_side_effects=True, vmem_limit_bytes=48 * 2**20
        ),
        cost_estimate=pl.CostEstimate(
            flops=4 * rows * tokens * width,
            bytes_accessed=8 * rows * width + 16 * rows * quarter + 4 * rows * tokens,
            transcendentals=rows * width,
        ),
        name="window_end",
    )(
        *(
            pltpu.with_memory_space_constraint(a, pltpu.HBM)
            for a in (acts, own, inner_weight[0], adam_first[0], adam_second[0], anchor, outer_momentum)
        )
    )
    new_inner, new_anchor, new_momentum, back = pl.pallas_call(
        write_out,
        out_shape=tuple(jax.ShapeDtypeStruct(r.shape, r.dtype) for r in results),
        in_specs=[anywhere] * 4,
        out_specs=(anywhere,) * 4,
        scratch_shapes=[dma((8,))],
        compiler_params=pltpu.CompilerParams(vmem_limit_bytes=2**20),
        name="write_out",
    )(*results)
    return (new_inner, new_anchor, new_momentum, jnp.swapaxes(back, 0, 1)[None])


def solution(mesh):
    placed = (
        P("rep", None, "fsdp"),
        P("rep", None, "fsdp"),
        P("rep", "fsdp", None),
        P("rep", "fsdp", None),
        P("rep", "fsdp", None),
        P("fsdp", "rep"),
        P("fsdp", "rep"),
    )
    return jax.shard_map(
        on_device,
        mesh=mesh,
        in_specs=placed,
        out_specs=(P("fsdp", None), P("fsdp", "rep"), P("fsdp", "rep"), P("rep", None, "fsdp")),
        check_vma=False,
    )
```

```python
import functools
import jax
import jax.numpy as jnp
from jax import lax
from jax.experimental import pallas as pl
from jax.experimental.pallas import tpu as pltpu
from jax.sharding import PartitionSpec as P

BETA_ONE = 0.9
BETA_TWO = 0.95
INNER_RATE = 0.1
DECAY = 0.1
EPSILON = 1e-08
OUTER_RATE = 0.7
OUTER_MU = 0.9

MESH = pl.DeviceIdType.MESH
F32 = jnp.float32
BF16 = jnp.bfloat16
UNIT = 128
HOPS = (3, 6, 9, 12, 15, 18)

ARRIVALS = (
    (0, 0, 0),
    (3, 0, 0),
    (1, 0, 0),
    (0, 3, 0),
    (0, 1, 0),
    (3, 1, 0),
    (0, 0, 1),
    (2, 0, 0),
    (3, 3, 0),
    (1, 1, 0),
    (1, 3, 0),
    (0, 1, 1),
    (1, 0, 1),
    (0, 2, 0),
    (2, 1, 0),
    (3, 0, 1),
    (0, 3, 1),
    (2, 3, 0),
    (2, 0, 1),
    (0, 2, 1),
    (3, 2, 0),
    (3, 1, 1),
    (1, 2, 0),
    (1, 1, 1),
    (1, 3, 1),
    (3, 3, 1),
    (3, 2, 1),
    (2, 2, 0),
    (2, 3, 1),
    (2, 1, 1),
    (1, 2, 1),
    (2, 2, 1),
)
LATER = 4
BEHIND = 3


def plan():
    when = {key: i for i, key in enumerate(ARRIVALS)}
    ready = sorted((max(when[a, b, h], when[b, a, h]), h, when[a, b, h]) for a, b, h in ARRIVALS)
    assert all(at <= i + BEHIND for i, (at, _, _) in enumerate(ready))
    return [ARRIVALS[i] for _, _, i in ready]


UNITS = plan()
N_UNITS = len(UNITS)
STEPWISE = 25

TAIL = max(HOPS[3], STEPWISE - N_UNITS + HOPS[5], 8)
EARLY = min(2 * TAIL, 2 * (N_UNITS - HOPS[5]) - 2)


def packed(values, j):
    words = []
    for first in (0, 16):
        word = 0
        for i, v in enumerate(values[first : first + 16]):
            word |= v << (2 * i)
        words.append(word - (1 << 32) if word >= 1 << 31 else word)
    word = jnp.where(j < 16, jnp.int32(words[0]), jnp.int32(words[1]))
    return lax.shift_right_logical(word, 2 * lax.rem(j, 16)) & 3


def forwards(key):
    a, b, h = key
    out = []
    if key == (0, 0, 0):
        out.append("z")
    if b == 0:
        if a == 0:
            out += ["f+", "f-"]
        elif (a, h) == (3, 0):
            out.append("f+")
        elif (a, h) == (1, 1):
            out.append("f-")
        out += ["s+", "s-"]
    elif (b, h) == (3, 0):
        out.append("s+")
    elif (b, h) == (1, 1):
        out.append("s-")
    return out + ["sib"]


SENDS = {}
for _key in ARRIVALS:
    for _way in forwards(_key):
        SENDS[_key, _way] = len(SENDS)
N_SENDS = len(SENDS)


def kernel(
    h_hbm, g_hbm, w_hbm, m_hbm, v_hbm, anchor_hbm, moment_hbm,
    inner_out, anchor_out, moment_out, back_out,
    grads, acts, weight, first_m, second_m, anchor, moment,
    stepped, from_near, from_far, inner, total, back,
    load_sem, block_recv, sib_recv, block_send,
    sum_send, near_recv, far_recv, part_recv, part_one, part_two, out_sem, last_sem,
):
    rep = lax.axis_index("rep")
    place = lax.axis_index("fsdp")
    core = lax.rem(place, 2)
    zh = lax.rem(lax.div(place, 2), 2)
    y = lax.rem(lax.div(place, 4), 4)
    x = lax.div(place, 16)

    def at(px, py, ph, pc):
        return ((px * 4 + py) * 2 + ph) * 2 + pc

    def moved(a, b):
        dx = a + core * (b - a)
        dy = b + core * (a - b)
        return lax.rem(x + dx, 4), lax.rem(y + dy, 4)

    def chip(a, b):
        return at(*moved(a, b), zh, core)

    ways = {
        "f+": (rep, chip(1, 0)),
        "f-": (rep, chip(3, 0)),
        "s+": (rep, chip(0, 1)),
        "s-": (rep, chip(0, 3)),
        "z": (rep, at(x, y, 1 - zh, core)),
        "sib": (rep, at(x, y, zh, 1 - core)),
    }

    loads = [
        pltpu.make_async_copy(src, dst, load_sem.at[i])
        for i, (src, dst) in enumerate(
            (
                (g_hbm, grads.at[pl.ds(pl.multiple_of(place * 64, 64), 64)]),
                (h_hbm, acts),
                (w_hbm, weight),
                (m_hbm, first_m),
                (v_hbm, second_m),
                (anchor_hbm, anchor),
                (moment_hbm, moment),
            )
        )
    ]
    barrier = pltpu.get_barrier_semaphore()
    for way in ways.values():
        pl.semaphore_signal(barrier, inc=1, device_id=way, device_id_type=MESH)

    for other in range(1, 4):
        pl.semaphore_signal(
            barrier, inc=1, device_id=(lax.rem(rep + other, 4), place), device_id_type=MESH
        )
    for load in loads:
        load.start()

    pl.semaphore_wait(barrier, 9)

    def unit_at(a, b, h):
        px, py = moved(a, b)
        ph = zh + h - 2 * zh * h
        return (px * 4 + py) * 2 + ph

    def block(unit, c):
        return grads.at[pl.ds(pl.multiple_of((unit * 2 + c) * 64, 64), 64)]

    def block_copy(key, way):
        unit = unit_at(*key)
        held = block(unit, core)
        recv = sib_recv if way == "sib" else block_recv
        return pltpu.make_async_remote_copy(
            src_ref=held,
            dst_ref=held,
            send_sem=block_send.at[SENDS[key, way]],
            recv_sem=recv.at[unit],
            device_id=ways[way],
            device_id_type=MESH,
        )

    def arrived(unit, c, sem):
        held = block(unit, c)
        pltpu.make_async_copy(held, held, sem.at[unit]).wait()

    def see_to(key):
        if key == (0, 0, 0):
            loads[0].wait()
        else:
            arrived(unit_at(*key), core, block_recv)
        for way in forwards(key):
            block_copy(key, way).start()

    def sum_copy(j, target):
        return [
            pltpu.make_async_remote_copy(
                src_ref=stepped.at[j],
                dst_ref=kept.at[j],
                send_sem=sum_send.at[j],
                recv_sem=recv.at[j],
                device_id=(target, place),
                device_id_type=MESH,
            )
            for kept, recv in ((from_near, near_recv), (from_far, far_recv))
        ]

    def part_copy(j, target, sems):
        return pltpu.make_async_remote_copy(
            src_ref=inner.at[j],
            dst_ref=inner.at[j],
            send_sem=sems.at[j],
            recv_sem=part_recv.at[j],
            device_id=(target, place),
            device_id_type=MESH,
        )

    def wait_on(ref, sem):
        pltpu.make_async_copy(ref, ref, sem).wait()

    def unit_of(j):
        a = packed([u[0] for u in UNITS], j)
        b = packed([u[1] for u in UNITS], j)
        h = packed([u[2] for u in UNITS], j)
        return unit_at(a, b, h)

    def columns(unit):
        return pl.ds(pl.multiple_of(unit * UNIT, UNIT), UNIT)

    def out_copy(j, unit):
        return pltpu.make_async_copy(inner.at[j], inner_out.at[:, columns(unit)], out_sem.at[j])

    def adamw(j, unit):
        weight_grad = lax.dot_general(
            acts[...],
            grads[columns(unit), :],
            (((1,), (1,)), ((), ())),
            preferred_element_type=F32,
        )
        cols = columns(unit)
        weight_full = weight[:, cols].astype(F32)
        first = BETA_ONE * first_m[:, cols].astype(F32) + (1.0 - BETA_ONE) * weight_grad
        second = (
            BETA_TWO * second_m[:, cols].astype(F32)
            + (1.0 - BETA_TWO) * weight_grad * weight_grad
        )
        bias_one = 1.0 - BETA_ONE**10
        bias_two = 1.0 - BETA_TWO**10
        update = (first * (1.0 / bias_one)) / (jnp.sqrt(second * (1.0 / bias_two)) + EPSILON)
        stepped[j] = (weight_full - INNER_RATE * (update + DECAY * weight_full)).astype(BF16)

    def input_grad(unit):
        rows = pl.ds(pl.multiple_of((unit // 2) * 256, 256), 256)
        for tile in range(4):
            cols = pl.ds(tile * 512, 512)
            total[:, cols] += jnp.dot(
                weight[:, rows], grads[rows, cols], preferred_element_type=F32
            )

    def roles(owner):
        low = owner < 2
        near = owner ^ 1
        return near, jnp.where(low, 2, 1), jnp.where(low, 3, 0)

    def outer(j, unit, owner, near, middle, stepwise):
        cols = pl.ds(pl.multiple_of((unit - owner * 8) * UNIT, UNIT), UNIT)
        wait_on(from_near.at[j], near_recv.at[j])

        @pl.when(jnp.logical_not(stepwise))
        def _():
            wait_on(from_far.at[j], far_recv.at[j])

        beyond = jnp.where(stepwise, 0.0, from_far[j].astype(F32))
        summed = stepped[j].astype(F32) + from_near[j].astype(F32) + beyond
        old = anchor[:, cols]
        delta = old - summed * 0.25
        moment_next = OUTER_MU * moment[:, cols] + delta
        anchor_next = old - OUTER_RATE * (delta + OUTER_MU * moment_next)
        inner[j] = anchor_next.astype(BF16)
        part_copy(j, near, part_one).start()

        @pl.when(jnp.logical_not(stepwise))
        def _():
            part_copy(j, middle, part_two).start()

        moment[:, cols] = moment_next
        anchor[:, cols] = anchor_next
        out_copy(j, unit).start()

    def line(j, unit):
        owner = unit >> 3
        stepwise = (j < STEPWISE) & ((owner == 0) | (owner == 3))
        return owner, *roles(owner), stepwise

    def first_hop(j, unit):
        owner, near, middle, far, stepwise = line(j, unit)

        @pl.when(rep == far)
        def _():
            sum_copy(j, middle)[0].start()

        @pl.when((rep == near) & jnp.logical_not(stepwise))
        def _():
            sum_copy(j, owner)[0].start()

    def add_to(j, kept, recv):
        wait_on(kept.at[j], recv.at[j])
        stepped[j] = (stepped[j].astype(F32) + kept[j].astype(F32)).astype(BF16)

    def take_part(j, unit):
        wait_on(inner.at[j], part_recv.at[j])
        out_copy(j, unit).start()

    def along_rep(t, units):
        for hop in range(6, 0, -1):
            j = t - HOPS[hop - 1]

            @pl.when((j >= 0) & (j < (STEPWISE if hop > 4 else N_UNITS)))
            def _():
                unit = units[HOPS[hop - 1] - 1]
                owner, near, middle, far, stepwise = line(j, unit)
                direct = jnp.logical_not(stepwise)
                if hop == 1:

                    @pl.when(rep == middle)
                    def _():
                        add_to(j, from_near, near_recv)
                        sum_copy(j, jnp.where(stepwise, near, owner))[1].start()

                if hop == 2:

                    @pl.when((rep == near) & stepwise)
                    def _():
                        add_to(j, from_far, far_recv)
                        sum_copy(j, owner)[0].start()

                if hop in (2, 3):

                    @pl.when((rep == owner) & (stepwise if hop == 3 else direct))
                    def _():
                        outer(j, unit, owner, near, middle, stepwise)

                if hop in (3, 4):

                    @pl.when((rep == near) & (stepwise if hop == 4 else direct))
                    def _():
                        take_part(j, unit)

                        @pl.when(stepwise)
                        def _():
                            part_copy(j, middle, part_one).start()

                if hop in (3, 5):

                    @pl.when((rep == middle) & (stepwise if hop == 5 else direct))
                    def _():
                        take_part(j, unit)
                        part_copy(j, far, part_one).start()

                if hop in (4, 6):

                    @pl.when((rep == far) & (stepwise if hop == 6 else direct))
                    def _():
                        take_part(j, unit)

    def step(t, units):
        for i, key in enumerate(ARRIVALS):

            @pl.when(t == i)
            def _():
                see_to(key)

        @pl.when(t == 0)
        def _():
            total[...] = jnp.zeros_like(total)

        @pl.when(t == BEHIND)
        def _():
            for load in loads[1:]:
                load.wait()

        j = t - BEHIND
        along_rep(j, units)
        unit = unit_of(jnp.minimum(jnp.maximum(j, 0), N_UNITS - 1))

        @pl.when((j >= 0) & (j < N_UNITS))
        def _():
            arrived(unit, 1 - core, sib_recv)
            adamw(j, unit)
            first_hop(j, unit)

        done = j - LATER
        second = packed([u[2] for u in UNITS], jnp.minimum(jnp.maximum(done, 0), N_UNITS - 1))

        @pl.when((done >= 0) & (done < N_UNITS) & (second == 1))
        def _():
            input_grad(units[LATER - 1])

        @pl.when(j == N_UNITS + LATER)
        def _():
            back[...] = total[...].astype(BF16)
            pltpu.make_async_copy(back, back_out, last_sem.at[0]).start()

        @pl.when(j == N_UNITS + HOPS[2] - 1)
        def _():
            pltpu.make_async_copy(anchor, anchor_out, last_sem.at[1]).start()
            pltpu.make_async_copy(moment, moment_out, last_sem.at[2]).start()

        @pl.when(j == N_UNITS + HOPS[1])
        def _():
            for key, way in SENDS:
                block_copy(key, way).wait_send()

        for half in range(2):
            old = 2 * (j - N_UNITS) + half

            @pl.when((old >= 0) & (old < EARLY))
            def _():
                finish(old, 0)

        return (unit, *units[:-1])

    def finish(j, carry):
        unit = unit_of(j)
        owner, near, middle, far, stepwise = line(j, unit)

        @pl.when(rep != owner)
        def _():
            sum_copy(j, owner)[0].wait_send()

        @pl.when((rep == owner) | (rep == middle) | ((rep == near) & stepwise))
        def _():
            part_copy(j, near, part_one).wait_send()

        @pl.when((rep == owner) & jnp.logical_not(stepwise))
        def _():
            part_copy(j, near, part_two).wait_send()

        out_copy(j, unit).wait()
        return carry

    lax.fori_loop(0, BEHIND + N_UNITS + TAIL, step, (jnp.int32(0),) * HOPS[5])
    lax.fori_loop(EARLY, N_UNITS, finish, 0)
    pltpu.make_async_copy(back, back_out, last_sem.at[0]).wait()
    pltpu.make_async_copy(anchor, anchor_out, last_sem.at[1]).wait()
    pltpu.make_async_copy(moment, moment_out, last_sem.at[2]).wait()


def write_out(*refs):
    sems = refs[8]
    copies = []
    for i in range(4):
        half = refs[i].shape[0] // 2
        for rows in (pl.ds(0, half), pl.ds(half, half)):
            copies.append(
                pltpu.make_async_copy(refs[i].at[rows], refs[4 + i].at[rows], sems.at[len(copies)])
            )
    for copy in copies:
        copy.start()
    for copy in copies:
        copy.wait()


def on_device(hidden, out_grad, inner_weight, adam_first, adam_second, anchor, outer_momentum):
    acts = jnp.swapaxes(hidden[0], 0, 1)
    own = jnp.swapaxes(out_grad[0], 0, 1)
    rows, tokens = acts.shape
    width = inner_weight.shape[2]
    quarter = anchor.shape[1]
    anywhere = pl.BlockSpec(memory_space=pl.ANY)
    dma = pltpu.SemaphoreType.DMA
    slots = (N_UNITS, rows, UNIT)
    results = pl.pallas_call(
        kernel,
        out_shape=(
            jax.ShapeDtypeStruct((rows, width), BF16),
            jax.ShapeDtypeStruct((rows, quarter), F32),
            jax.ShapeDtypeStruct((rows, quarter), F32),
            jax.ShapeDtypeStruct((rows, tokens), BF16),
        ),
        in_specs=[anywhere] * 7,
        out_specs=(anywhere,) * 4,
        scratch_shapes=[
            pltpu.VMEM((width, tokens), BF16),
            pltpu.VMEM((rows, tokens), BF16),
            pltpu.VMEM((rows, width), BF16),
            pltpu.VMEM((rows, width), BF16),
            pltpu.VMEM((rows, width), BF16),
            pltpu.VMEM((rows, quarter), F32),
            pltpu.VMEM((rows, quarter), F32),
            pltpu.VMEM(slots, BF16),
            pltpu.VMEM(slots, BF16),
            pltpu.VMEM(slots, BF16),
            pltpu.VMEM(slots, BF16),
            pltpu.VMEM((rows, tokens), F32),
            pltpu.VMEM((rows, tokens), BF16),
            dma((7,)),
            dma((N_UNITS,)),
            dma((N_UNITS,)),
            dma((N_SENDS,)),
            dma((N_UNITS,)),
            dma((N_UNITS,)),
            dma((N_UNITS,)),
            dma((N_UNITS,)),
            dma((N_UNITS,)),
            dma((N_UNITS,)),
            dma((N_UNITS,)),
            dma((3,)),
        ],
        compiler_params=pltpu.CompilerParams(
            collective_id=0, has_side_effects=True, vmem_limit_bytes=48 * 2**20
        ),
        cost_estimate=pl.CostEstimate(
            flops=4 * rows * tokens * width,
            bytes_accessed=8 * rows * width + 16 * rows * quarter + 4 * rows * tokens,
            transcendentals=rows * width,
        ),
        name="window_end",
    )(
        *(
            pltpu.with_memory_space_constraint(a, pltpu.HBM)
            for a in (acts, own, inner_weight[0], adam_first[0], adam_second[0], anchor, outer_momentum)
        )
    )
    new_inner, new_anchor, new_momentum, back = pl.pallas_call(
        write_out,
        out_shape=tuple(jax.ShapeDtypeStruct(r.shape, r.dtype) for r in results),
        in_specs=[anywhere] * 4,
        out_specs=(anywhere,) * 4,
        scratch_shapes=[dma((8,))],
        compiler_params=pltpu.CompilerParams(vmem_limit_bytes=2**20),
        name="write_out",
    )(*results)
    return (new_inner, new_anchor, new_momentum, jnp.swapaxes(back, 0, 1)[None])


def solution(mesh):
    placed = (
        P("rep", None, "fsdp"),
        P("rep", None, "fsdp"),
        P("rep", "fsdp", None),
        P("rep", "fsdp", None),
        P("rep", "fsdp", None),
        P("fsdp", "rep"),
        P("fsdp", "rep"),
    )
    return jax.shard_map(
        on_device,
        mesh=mesh,
        in_specs=placed,
        out_specs=(P("fsdp", None), P("fsdp", "rep"), P("fsdp", "rep"), P("rep", None, "fsdp")),
        check_vma=False,
    )
```
